32 devices in a mesh: pipe: 8 (over y, x, core), dp: 4 (over z).
Axes of the slice: x: 2, y: 2, z: 4, core: 2. Of those that a mesh axis runs over, the one named last changes fastest.
Arguments:
- x_saved: bfloat16 [8, 1024, 1024], P('pipe', 'dp'), may hold values from -6 to 6
- up_weights: bfloat16 [8, 1024, 2048], P('pipe', 'dp'), may hold values from -0.1875 to 0.1875
- down_weights: bfloat16 [8, 2048, 1024], P('pipe', 'dp'), may hold values from -0.125 to 0.125
- norm_gain: float32 [8, 1024], P('pipe'), may hold values from 0.1 to 1.9
- layer_scale: float32 [8, 1024], P('pipe'), may hold values from 0.1 to 1
- cotangent: bfloat16 [1024, 1024], P('dp'), may hold values from -0.119628906 to 0.119628906
- lengths: int32 [4, 2], P('dp'), may hold values from 1 to 128, 160 in all within a row
Outputs:
- weight_grad: bfloat16 [8, 2048, 1024], P('pipe', 'dp')
- gain_grad: float32 [8, 1024], P('pipe')
- scale_grad: float32 [8, 1024], P('pipe')
The draws below stay inside these ranges and needn't reach their ends.
Inputs may be any that keep to these rules, and one draw needn't show every extreme that they name: `lengths`: each row sums to 128 * M * 5 // 8.
All inputs are finite; a program needn't handle non-finite values.
Results may differ from the reference program's by a relative error of at most 0.04.
Values may be sent and summed in bfloat16 or wider, within the bound.
No kernel may reach another device: no remote copies, remote signals or barrier semaphores. Data moves between devices by JAX's collectives and lax.ppermute only.
A program may use at most 64 MiB of HBM per device.

```python
import math
import jax
import jax.numpy as jnp
import numpy as np
from jax import lax

D = 1024
FF = 2048
M = 2
SLOT = 128
LAYERS = 8
UTTS = 4
TOKENS = 1024
N_DP = 4


def spiked(array, stream_key, source, target, blocks, factor):
    owner, partner = [(jnp.arange(array.shape[dim]) // (array.shape[dim] // blocks)).reshape([-1 if axis == dim else 1 for axis in range(array.ndim)]) for dim in (source, target)]
    chosen = jax.random.permutation(stream_key, blocks)[partner]
    strong = (owner == chosen) | (owner == (partner + blocks // 2) % blocks)
    return jnp.where(strong, factor * array, array)


def shard_levels(rng, extent, split, least, top_value):
    gain, own = 1.0, jax.random.fold_in(rng, 6)
    for dim, blocks in split:
        draws = jnp.exp(jax.random.uniform(jax.random.fold_in(own, dim), (blocks,), jnp.float32, least / len(split), top_value / len(split)))
        gain = gain * jnp.repeat(draws, extent[dim] // blocks).reshape([-1 if axis == dim else 1 for axis in range(len(extent))])
    return gain


def profile(number_of, total, reach, lean):
    loads = [(1 << 20) // math.isqrt(grade ** lean) + 1 for grade in range(2, number_of + 1)]
    spare, holding = total - reach - (number_of - 1), [1] * (number_of - 1)
    while spare > 0:
        free = [i for i in range(number_of - 1) if holding[i] < reach]
        mass, budget = sum([loads[i] for i in free]), spare
        for i in free:
            extra = min(reach - holding[i], max(1, budget * loads[i] // mass), spare)
            holding[i] = holding[i] + extra
            spare = spare - extra
    return np.array([reach] + holding)


def ragged(stream_key, count, total, reach, lean):
    if count == 2:
        one = jax.random.randint(stream_key, (), max(1, total - reach), min(reach, total - 1) + 1)
        return jnp.stack([one, total - one])
    sizes = jnp.asarray(profile(count, total, reach, lean), jnp.int32)
    pairs = (count - 1) // 2
    source_of, sink = sizes[1:1 + 2 * pairs:2], sizes[2:2 + 2 * pairs:2]
    margin = jnp.minimum(source_of - 1, reach - sink)
    shifted = jax.random.randint(jax.random.fold_in(stream_key, 1), (pairs,), 0, 1 << 20) % (margin + 1)
    sizes = sizes.at[1:1 + 2 * pairs:2].set(source_of - shifted).at[2:2 + 2 * pairs:2].set(sink + shifted)
    return sizes[jax.random.permutation(jax.random.fold_in(stream_key, 2), count)]


def scatter_about(rng, shape, width, most, shards=(), held_as=jnp.bfloat16):
    entries = jax.random.normal(rng, shape, jnp.float32) * width
    if len(shards) > 0:
        entries = shard_levels(rng, shape, shards, -0.22, 0.18) * entries
    return jnp.clip(entries, min=-most, max=most).astype(held_as)


def noise_with(rng, shape, spread, limit, shards, heavy, held_as=jnp.bfloat16):
    drawn = spread * jax.random.normal(rng, shape, jnp.float32)
    if shards:
        drawn = drawn * shard_levels(rng, shape, shards, -0.22, 0.18)
    return jnp.clip(spiked(drawn, jax.random.fold_in(rng, 3), *heavy), -limit, limit).astype(held_as)


def setup_inputs(seed: int = 0) -> dict:
    key_list = jax.random.split(jax.random.key(seed), 8)
    x_saved = noise_with(key_list[0], (LAYERS, TOKENS, D), 1.0, 6.0, ((0, 8), (1, 4)), (1, 2, 4, 2.0))
    up_weights = scatter_about(key_list[1], (LAYERS, D, FF), D ** -0.5, 0.1875, ((0, 8), (1, 4)))
    down_weights = scatter_about(key_list[2], (LAYERS, FF, D), FF ** -0.5, 0.125, ((0, 8), (1, 4)))
    norm_gain = jnp.clip(1.0 + 0.18 * jax.random.normal(key_list[3], (LAYERS, D), jnp.float32), 0.1, 1.9)
    layer_scale = jnp.clip(jnp.exp(math.log(1.0) - 2.3025851 * jax.random.uniform(key_list[4], (LAYERS, D), jnp.float32) ** shard_levels(key_list[4], (LAYERS, D), ((0, 8),), -0.2, 0.2)), 0.1, 1.0)
    cotangent = scatter_about(key_list[5], (TOKENS, D), 0.02, 0.119628906, ((0, 4),))
    lengths = jax.vmap(lambda own: ragged(own, M, SLOT * M * 5 // 8, SLOT, 0))(jax.random.split(key_list[6], UTTS)).reshape((UTTS, M)).astype(jnp.int32)
    return {"x_saved": x_saved, "up_weights": up_weights, "down_weights": down_weights, "norm_gain": norm_gain, "layer_scale": layer_scale, "cotangent": cotangent, "lengths": lengths}


epsilon = 1e-06

def gelu_tanh(values):
    return jax.nn.gelu(values, approximate=True)

def layer_back(x_rows, incoming, up_weight, down_weight, gain_vec, scale_vec):
    x_float = x_rows.astype(jnp.float32)
    inverse = lax.rsqrt(lax.optimization_barrier(jnp.mean(x_float * x_float, axis=-1, keepdims=True)) + epsilon)
    unit = x_float * inverse
    normed = (unit * gain_vec).astype(jnp.bfloat16)
    hidden = jnp.dot(normed, up_weight, preferred_element_type=jnp.float32)
    active, gelu_back = jax.vjp(gelu_tanh, hidden)
    act = active.astype(jnp.bfloat16)
    branch = jnp.dot(act, down_weight, preferred_element_type=jnp.float32)
    upper = incoming.astype(jnp.float32)
    scale_part = lax.optimization_barrier(jnp.sum(upper * branch, axis=0))
    branch_grad = (upper * scale_vec).astype(jnp.bfloat16)
    act_grad = jnp.dot(branch_grad, down_weight.T, preferred_element_type=jnp.float32)
    hidden_grad = gelu_back(act_grad)[0].astype(jnp.bfloat16)
    normed_grad = jnp.dot(hidden_grad, up_weight.T, preferred_element_type=jnp.float32)
    gain_part = lax.optimization_barrier(jnp.sum(normed_grad * unit, axis=0))
    unit_grad = normed_grad * gain_vec
    back_rows = (upper + inverse * (unit_grad - unit * lax.optimization_barrier(jnp.mean(unit_grad * unit, axis=-1, keepdims=True)))).astype(jnp.bfloat16)
    return (act, branch_grad, back_rows, gain_part, scale_part)

def reference(x_saved, up_weights, down_weights, norm_gain, layer_scale, cotangent, lengths):
    token_ids = jnp.arange(TOKENS, dtype=jnp.int32)
    position = token_ids % SLOT
    owner = token_ids // SLOT
    valid = position < lengths.reshape(-1)[owner]
    start_grad = jnp.where(valid[:, None], cotangent, jnp.zeros_like(cotangent))

    def one_layer(incoming, layer):
        x_rows, up_weight, down_weight, gain_vec, scale_vec = layer
        act, branch_grad, back_rows, gain_part, scale_part = layer_back(x_rows, incoming, up_weight, down_weight, gain_vec, scale_vec)
        act_split = act.reshape(N_DP, -1, FF)
        grad_split = branch_grad.reshape(N_DP, -1, D)

        def partial_of(pair):
            return lax.dot_general(pair[0], pair[1], (((0,), (0,)), ((), ())), preferred_element_type=jnp.float32).astype(jnp.bfloat16)
        partials = lax.map(partial_of, (act_split, grad_split))
        partials = lax.optimization_barrier(partials)
        weight_part = lax.optimization_barrier(jnp.sum(partials.astype(jnp.float32), axis=0)).astype(jnp.bfloat16)
        return (back_rows, (weight_part, gain_part, scale_part))
    unused, outputs = lax.scan(one_layer, start_grad, (x_saved, up_weights, down_weights, norm_gain, layer_scale), reverse=True)
    return (outputs[0], outputs[1], outputs[2])
```

```python
import functools
import math

import jax
import jax.numpy as jnp
from jax import lax
from jax.experimental import pallas as pl
from jax.experimental.pallas import tpu as pltpu
from jax.sharding import PartitionSpec as P

epsilon = 1e-06
slope = math.sqrt(2.0 / math.pi)
cubic = 0.044715
NT = (((1,), (1,)), ((), ()))
axes = ("pipe", "dp")
in_vmem = pl.BlockSpec(memory_space=pltpu.VMEM)
in_smem = pl.BlockSpec(memory_space=pltpu.SMEM)


def held(array):
    return pltpu.with_memory_space_constraint(array, pltpu.VMEM)


def home_of(section, lines):
    middle = lines // 2
    return middle if ((section + 1) // 2) % 2 == 0 else max(middle - 1, 0)


def hidden_kernel(parts, piece_rows, x_ref, gain_ref, *refs):
    up_refs, (act_ref, slope_ref) = refs[:parts], refs[parts:]
    depth, wide = up_refs[0].shape
    chunk = math.gcd(wide, 512)

    @pl.loop(0, x_ref.shape[0] // piece_rows)
    def piece(index):
        rows = pl.ds(pl.multiple_of(index * piece_rows, piece_rows), piece_rows)
        x = x_ref[rows, :].astype(jnp.float32)
        inverse = lax.rsqrt(jnp.mean(x * x, axis=-1, keepdims=True) + epsilon)
        normed = (x * inverse * gain_ref[...]).astype(jnp.bfloat16)
        for start in range(0, wide, chunk):
            hidden = jnp.zeros((piece_rows, chunk), jnp.float32)
            for part in range(parts):
                hidden += jnp.dot(
                    normed[:, part * depth : (part + 1) * depth],
                    up_refs[part][:, start : start + chunk],
                    preferred_element_type=jnp.float32,
                )
            square = hidden * hidden
            bent = jnp.tanh(slope * hidden * (1.0 + cubic * square))
            half = 0.5 + 0.5 * bent
            act_ref[rows, start : start + chunk] = (hidden * half).astype(jnp.bfloat16)
            rise = half + (0.5 * slope) * hidden * (1.0 - bent * bent) * (1.0 + (3.0 * cubic) * square)
            slope_ref[rows, start : start + chunk] = rise.astype(jnp.bfloat16)


def chain_kernel(parts, piece_rows, plan_ref, recv_ref, x_ref, slope_ref, gain_ref, scale_ref, *refs):
    up_refs, down_refs = refs[:parts], refs[parts : 2 * parts]
    store_in, total_in, back_ref, store_ref, total_ref = refs[2 * parts :]
    width = x_ref.shape[1]

    @pl.when(plan_ref[1] == 1)
    def active():
        rows = pl.ds(pl.multiple_of(plan_ref[0] * piece_rows, piece_rows), piece_rows)

        @pl.when(plan_ref[2] == 0)
        def received():
            store_ref[rows, :] = recv_ref[...]

        upper = store_ref[rows, :].astype(jnp.float32)
        branch_grad = (upper * scale_ref[...]).astype(jnp.bfloat16)
        pieces = []
        for part in range(parts):
            block = down_refs[part].shape[0]
            grown = lax.dot_general(branch_grad, down_refs[part][...], NT, preferred_element_type=jnp.float32)
            rise = slope_ref[rows, part * block : (part + 1) * block].astype(jnp.float32)
            pieces.append((grown * rise).astype(jnp.bfloat16))
        hidden_grad = jnp.concatenate(pieces, axis=1)
        x = x_ref[rows, :].astype(jnp.float32)
        inverse = lax.rsqrt(jnp.mean(x * x, axis=-1, keepdims=True) + epsilon)
        unit = x * inverse
        normed_grad = jnp.concatenate(
            [
                lax.dot_general(hidden_grad, up_refs[part][...], NT, preferred_element_type=jnp.float32)
                for part in range(parts)
            ],
            axis=1,
        )
        total_ref[...] += jnp.sum(normed_grad * unit, axis=0, keepdims=True)
        unit_grad = normed_grad * gain_ref[...]
        mean = jnp.sum(unit_grad * unit, axis=-1, keepdims=True) * (1.0 / width)
        back_ref[...] = (upper + inverse * (unit_grad - unit * mean)).astype(jnp.bfloat16)


def shards(x_saved, up_weights, down_weights, norm_gain, layer_scale, cotangent, lengths):
    sections, lines = lax.axis_size("pipe"), lax.axis_size("dp")
    section, line = lax.axis_index("pipe"), lax.axis_index("dp")
    row_count, width = cotangent.shape
    wide = up_weights.shape[2]
    batches = lengths.shape[1]
    slot_rows = row_count // batches
    piece_rows = row_count * 5 // 8
    gain, scale = norm_gain, layer_scale

    def device(p, z):
        return p * lines + z

    def home(p):
        return home_of(p, lines)

    def to_home(array, source, layers):
        return lax.ppermute(array, axes, [(device(p, source), device(p, home(p))) for p in layers])

    def from_home(array, target):
        return lax.ppermute(array, axes, [(device(p, home(p)), device(p, target)) for p in range(sections)])

    ends = jnp.cumsum(lengths[0])
    pack_ids = jnp.arange(piece_rows, dtype=jnp.int32)
    owner = jnp.sum(pack_ids[:, None] >= ends[None, :], axis=1)
    starts = ends - lengths[0]
    chosen = owner[:, None] == jnp.arange(batches, dtype=jnp.int32)[None, :]
    offset = jnp.sum(jnp.where(chosen, starts[None, :], 0), axis=1)
    source_row = owner * slot_rows + pack_ids - offset
    picker = (source_row[:, None] == jnp.arange(row_count, dtype=jnp.int32)[None, :]).astype(jnp.bfloat16)

    def packed(rows):
        return jnp.dot(picker, rows, preferred_element_type=jnp.float32).astype(jnp.bfloat16)

    every = range(sections)
    x_pack, start_pack = packed(x_saved[0]), packed(cotangent)
    x_all = jnp.concatenate([to_home(x_pack, z, every) for z in range(lines)], axis=0)
    ups = [to_home(up_weights[0], z, every) for z in range(lines)]
    store = jnp.concatenate([to_home(start_pack, z, [sections - 1]) for z in range(lines)], axis=0)
    downs = [to_home(down_weights[0], z, every) for z in range(lines)]

    x_held, up_held, down_held = held(x_all), [held(u) for u in ups], [held(d) for d in downs]
    total_rows = lines * piece_rows
    act, rise = pl.pallas_call(
        functools.partial(hidden_kernel, lines, piece_rows),
        out_shape=[jax.ShapeDtypeStruct((total_rows, wide), jnp.bfloat16)] * 2,
        in_specs=[in_vmem] * (2 + lines),
        out_specs=[in_vmem] * 2,
        compiler_params=pltpu.CompilerParams(vmem_limit_bytes=16 << 20),
        name="hidden",
    )(x_held, gain, *up_held)
    rise = held(rise)

    total = jnp.zeros((1, width), jnp.float32)
    received = jnp.zeros((piece_rows, width), jnp.bfloat16)
    first = (section == sections - 1).astype(jnp.int32)
    at_home = jnp.zeros((), jnp.bool_)
    for p in every:
        at_home = jnp.logical_or(at_home, jnp.logical_and(section == p, line == home(p)))
    steps = sections + lines - 1
    chain = pl.pallas_call(
        functools.partial(chain_kernel, lines, piece_rows),
        out_shape=[
            jax.ShapeDtypeStruct((piece_rows, width), jnp.bfloat16),
            jax.ShapeDtypeStruct((total_rows, width), jnp.bfloat16),
            jax.ShapeDtypeStruct((1, width), jnp.float32),
        ],
        in_specs=[in_smem] + [in_vmem] * (7 + 2 * lines),
        out_specs=[in_vmem] * 3,
        input_output_aliases={6 + 2 * lines: 1, 7 + 2 * lines: 2},
        compiler_params=pltpu.CompilerParams(vmem_limit_bytes=16 << 20),
        name="chain",
    )
    for step in range(steps):
        piece = step - (sections - 1 - section)
        working = jnp.logical_and(at_home, jnp.logical_and(piece >= 0, piece < lines))
        plan = jnp.stack([jnp.clip(piece, 0, lines - 1), working.astype(jnp.int32), first])
        back, store, total = chain(
            plan, held(received), x_held, rise, gain, scale, *up_held, *down_held, held(store), held(total)
        )
        moving = [p for p in range(1, sections) if 0 <= step - (sections - 1 - p) < lines]
        if moving:
            received = lax.ppermute(
                back, axes, [(device(p, home(p)), device(p - 1, home(p - 1))) for p in moving]
            )

    block = wide // lines
    scale_part = jnp.zeros((1, width), jnp.float32)
    weight_part = None
    for z in range(lines):
        grown = lax.dot_general(
            act[:, z * block : (z + 1) * block], store, (((0,), (0,)), ((), ())), preferred_element_type=jnp.float32
        )
        scale_part += jnp.sum(grown * downs[z].astype(jnp.float32), axis=0, keepdims=True)
        moved = from_home((grown * scale).astype(jnp.bfloat16), z)
        weight_part = moved if weight_part is None else weight_part + moved
    sums = jnp.concatenate([total, scale_part], axis=0)
    spread = sum(from_home(sums, z) for z in range(lines))
    return (weight_part[None], spread[0:1], spread[1:2])


def solution(mesh):
    return jax.shard_map(
        shards,
        mesh=mesh,
        in_specs=(
            P("pipe", "dp", None),
            P("pipe", "dp", None),
            P("pipe", "dp", None),
            P("pipe", None),
            P("pipe", None),
            P("dp", None),
            P("dp", None),
        ),
        out_specs=(P("pipe", "dp", None), P("pipe", None), P("pipe", None)),
        check_vma=False,
    )
```

```python
import functools
import math

import jax
import jax.numpy as jnp
from jax import lax
from jax.experimental import pallas as pl
from jax.experimental.pallas import tpu as pltpu
from jax.sharding import PartitionSpec as P

epsilon = 1e-06
slope = math.sqrt(2.0 / math.pi)
cubic = 0.044715
NN = (((1,), (0,)), ((), ()))
NT = (((1,), (1,)), ((), ()))
TN = (((0,), (0,)), ((), ()))
axes = ("pipe", "dp")
skew = 2
in_vmem = pl.BlockSpec(memory_space=pltpu.VMEM)
anywhere = pl.BlockSpec(memory_space=pl.ANY)
in_smem = pl.BlockSpec(memory_space=pltpu.SMEM)
tail_rows = 16


def held(array):
    return pltpu.with_memory_space_constraint(array, pltpu.VMEM)


def dot(a, b, dims):
    return lax.dot_general(a, b, dims, preferred_element_type=jnp.float32)


def bf16(shape):
    return jax.ShapeDtypeStruct(shape, jnp.bfloat16)


def home_of(section, lines):
    middle = lines // 2
    return middle if ((section + 1) // 2) % 2 == 0 else max(middle - 1, 0)


def span(index, size):
    return pl.ds(pl.multiple_of(index * size, size), size)


def pack_kernel(lengths_ref, x_in, start_in, up_in, out_ref, x_ref, start_ref, sems):
    batches, (row_count, width) = lengths_ref.shape[1], x_ref.shape
    depth, wide = up_in.shape
    folds = wide // width
    rows = (out_ref.shape[0] - folds * depth) // 2
    copies = [
        pltpu.make_async_copy(x_in, x_ref, sems.at[0]),
        pltpu.make_async_copy(start_in, start_ref, sems.at[1]),
    ]
    for fold in range(folds):
        source = up_in.at[:, fold * width : (fold + 1) * width]
        target = out_ref.at[pl.ds(2 * rows + fold * depth, depth)]
        copies.append(pltpu.make_async_copy(source, target, sems.at[2 + fold]))
    for copy in copies:
        copy.start()
    slot_rows = row_count // batches
    packed = lax.broadcasted_iota(jnp.int32, (rows, row_count), 0)
    source = lax.broadcasted_iota(jnp.int32, (rows, row_count), 1)
    before = jnp.int32(0)
    wanted = packed
    for m in range(batches):
        wanted = jnp.where(packed >= before, packed - before + m * slot_rows, wanted)
        before = before + lengths_ref[0, m]
    picker = jnp.where(source == wanted, 1.0, 0.0).astype(jnp.bfloat16)
    for copy in copies:
        copy.wait()
    out_ref[:rows, :] = dot(picker, x_ref[...], NN).astype(jnp.bfloat16)
    out_ref[rows : 2 * rows, :] = dot(picker, start_ref[...], NN).astype(jnp.bfloat16)


def hidden_kernel(lines, rows, plan_ref, gain_ref, *refs):
    part_refs, (act_ref, rise_ref, x_all_ref, store_ref, turned_ref, up_ref, normed_ref, sems) = refs[:lines], refs[lines:]
    width, wide = up_ref.shape
    depth, folds = width // lines, wide // width
    chunk = math.gcd(wide, 512)
    line = plan_ref[2]
    copies = []
    for part in range(lines):
        shard = lax.rem(line + part, lines)
        place, deep = span(shard, rows), span(shard, depth)
        moves = [
            (part_refs[part].at[:rows], x_all_ref.at[place]),
            (part_refs[part].at[rows : 2 * rows], store_ref.at[place]),
        ]
        for fold in range(folds):
            source = part_refs[part].at[2 * rows + fold * depth : 2 * rows + (fold + 1) * depth]
            moves.append((source, up_ref.at[deep, fold * width : (fold + 1) * width]))
        for index, (source, target) in enumerate(moves):
            copies.append(pltpu.make_async_copy(source, target, sems.at[part, index]))
    for copy in copies:
        copy.start()
    for copy in copies:
        copy.wait()

    @pl.loop(0, lines)
    def piece(index):
        place = span(index, rows)
        x = x_all_ref[place, :].astype(jnp.float32)
        inverse = lax.rsqrt(jnp.mean(x * x, axis=-1, keepdims=True) + epsilon)
        normed_ref[...] = (x * inverse * gain_ref[...]).astype(jnp.bfloat16)
        for start in range(0, wide, chunk):
            columns = slice(start, start + chunk)
            hidden = dot(normed_ref[...], up_ref[:, columns], NN)
            square = hidden * hidden
            bent = jnp.tanh(slope * hidden * (1.0 + cubic * square))
            half = 0.5 + 0.5 * bent
            act_ref[place, columns] = (hidden * half).astype(jnp.bfloat16)
            rise = half + (0.5 * slope) * hidden * (1.0 - bent * bent) * (1.0 + (3.0 * cubic) * square)
            rise_ref[place, columns] = rise.astype(jnp.bfloat16)

    for start in range(0, wide, chunk):
        turned_ref[start : start + chunk, :] = up_ref[:, start : start + chunk].T


def turn_kernel(part, lines, plan_ref, turned_in, part_ref, turned_ref, flat_ref, sem):
    block = flat_ref.shape[0]
    copy = pltpu.make_async_copy(part_ref, flat_ref, sem)
    copy.start()
    copy.wait()
    turned_ref[:, span(lax.rem(plan_ref[2] + part, lines), block)] = flat_ref[...].T


def chain_kernel(step, rows, plan_ref, recv_ref, gain_ref, scale_ref, x_ref, rise_ref, up_ref, down_ref, *refs):
    store_in, total_in, back_ref, store_ref, total_ref, hidden_grad_ref, normed_grad_ref = refs
    width, wide = down_ref.shape
    piece = step - plan_ref[0]

    @pl.when(jnp.logical_and(piece >= 0, piece < x_ref.shape[0] // rows))
    def active():
        place = span(piece, rows)

        @pl.when(plan_ref[1] == 0)
        def received():
            store_ref[place, :] = recv_ref[...]

        upper = store_ref[place, :].astype(jnp.float32)
        branch_grad = (upper * scale_ref[...]).astype(jnp.bfloat16)
        chunk = math.gcd(wide, 512)
        for start in range(0, wide, chunk):
            grown = dot(branch_grad, down_ref[:, start : start + chunk], NN)
            rise = rise_ref[place, start : start + chunk].astype(jnp.float32)
            hidden_grad_ref[:, start : start + chunk] = (grown * rise).astype(jnp.bfloat16)
        hidden_grad = hidden_grad_ref[...]
        chunk = math.gcd(width, 256)
        for start in range(0, width, chunk):
            normed_grad_ref[:, start : start + chunk] = dot(hidden_grad, up_ref[:, start : start + chunk], NN)
        x = x_ref[place, :].astype(jnp.float32)
        inverse = lax.rsqrt(jnp.mean(x * x, axis=-1, keepdims=True) + epsilon)
        unit = x * inverse
        normed_grad = normed_grad_ref[...]
        lean = normed_grad * unit
        total_ref[...] += jnp.sum(lean, axis=0, keepdims=True)
        mean = jnp.sum(lean * gain_ref[...], axis=-1, keepdims=True) * (1.0 / width)
        back_ref[...] = (upper + inverse * (normed_grad * gain_ref[...] - unit * mean)).astype(jnp.bfloat16)


def weight_kernel(lines, plan_ref, scale_ref, total_ref, act_ref, store_ref, *refs):
    down_refs, out_refs, (down_ref, sems) = refs[:lines], refs[lines : 2 * lines], refs[2 * lines :]
    line = plan_ref[2]
    block, width = down_refs[0].shape
    copies = [pltpu.make_async_copy(down_refs[part], down_ref.at[part], sems.at[part]) for part in range(lines)]
    for copy in copies:
        copy.start()
    scale_part = jnp.zeros((1, width), jnp.float32)
    for part in range(lines):
        columns = span(lax.rem(line + part, lines), block)
        grown = dot(act_ref[:, columns], store_ref[...], TN)
        out_refs[part][:block, :] = (grown * scale_ref[...]).astype(jnp.bfloat16)
        copies[part].wait()
        scale_part += jnp.sum(grown * down_ref[part].astype(jnp.float32), axis=0, keepdims=True)
    lines_out = []
    for value in (total_ref[...], scale_part):
        high = value.astype(jnp.bfloat16).astype(jnp.float32)
        middle = (value - high).astype(jnp.bfloat16).astype(jnp.float32)
        lines_out += [high, middle, value - high - middle]
    lines_out.append(jnp.zeros((tail_rows - len(lines_out), width), jnp.float32))
    tail = jnp.concatenate(lines_out, axis=0).astype(jnp.bfloat16)
    for part in range(lines):
        out_refs[part][block:, :] = tail


def shards(x_saved, up_weights, down_weights, norm_gain, layer_scale, cotangent, lengths):
    sections, lines = lax.axis_size("pipe"), lax.axis_size("dp")
    section, line = lax.axis_index("pipe"), lax.axis_index("dp")
    row_count, width = cotangent.shape
    wide = up_weights.shape[2]
    block = down_weights.shape[1]
    rows = row_count * 5 // 8
    total_rows = lines * rows
    splits = 1
    piece_rows = rows // splits
    pieces = lines * splits
    steps = pieces + skew * (sections - 1)
    every = range(sections)

    def device(p, z):
        return p * lines + z

    def home(p):
        return home_of(p, lines)

    def route(p, part):
        return device(p, (home(p) + part) % lines), device(p, home(p))

    def to_home(array, after=None):
        parts = [array]
        for part in range(1, lines):
            sent = array if after is None else lax.optimization_barrier((array, after[part]))[0]
            parts.append(lax.ppermute(sent, axes, [route(p, part) for p in every]))
        return [pltpu.with_memory_space_constraint(array, pltpu.HBM) for array in parts]

    def from_home(array, part):
        return lax.ppermute(array, axes, [route(p, part)[::-1] for p in every])

    def call(kernel, name, outs, ins, scratch=(), aliases={}, limit=16 << 20, loose=()):
        specs = [in_smem if a.dtype == jnp.int32 else in_vmem for a in ins]
        fixed = [a if a.dtype == jnp.int32 else held(a) for a in ins]
        return pl.pallas_call(
            kernel,
            out_shape=outs,
            in_specs=specs + [anywhere] * len(loose),
            out_specs=[in_vmem] * len(outs),
            scratch_shapes=list(scratch),
            input_output_aliases=aliases,
            compiler_params=pltpu.CompilerParams(vmem_limit_bytes=limit),
            name=name,
        )(*fixed, *loose)

    at_home = jnp.zeros((), jnp.bool_)
    for p in every:
        at_home = jnp.logical_or(at_home, jnp.logical_and(section == p, line == home(p)))
    begin = jnp.where(at_home, skew * (sections - 1 - section), steps)
    plan = jnp.stack([begin, section == sections - 1, line]).astype(jnp.int32)

    (pack,) = call(
        pack_kernel,
        "pack",
        [bf16((2 * rows + up_weights.shape[1] * (wide // width), width))],
        [lengths],
        scratch=[pltpu.VMEM((row_count, width), jnp.bfloat16)] * 2 + [pltpu.SemaphoreType.DMA((2 + wide // width,))],
        loose=[x_saved[0], cotangent, up_weights[0]],
    )
    packs = to_home(pack)
    downs = to_home(down_weights[0], after=packs)

    act, rise, x_all, store, up_turned = call(
        functools.partial(hidden_kernel, lines, rows),
        "hidden",
        [bf16((total_rows, wide))] * 2 + [bf16((total_rows, width))] * 2 + [bf16((wide, width))],
        [plan, norm_gain],
        scratch=[
            pltpu.VMEM((width, wide), jnp.bfloat16),
            pltpu.VMEM((rows, width), jnp.bfloat16),
            pltpu.SemaphoreType.DMA((lines, 2 + wide // width)),
        ],
        loose=packs,
    )
    down_turned = jnp.zeros((width, wide), jnp.bfloat16)
    for part in range(lines):
        (down_turned,) = call(
            functools.partial(turn_kernel, part, lines),
            "turn",
            [bf16((width, wide))],
            [plan, down_turned],
            scratch=[pltpu.VMEM((block, width), jnp.bfloat16), pltpu.SemaphoreType.DMA],
            aliases={1: 0},
            loose=[downs[part]],
        )

    total = jnp.zeros((1, width), jnp.float32)
    arrived = [jnp.zeros((piece_rows, width), jnp.bfloat16)] * skew
    for step in range(steps):
        back, store, total = call(
            functools.partial(chain_kernel, step, piece_rows),
            "chain",
            [bf16((piece_rows, width)), bf16((total_rows, width)), jax.ShapeDtypeStruct((1, width), jnp.float32)],
            [plan, arrived.pop(0), norm_gain, layer_scale, x_all, rise, up_turned, down_turned, store, total],
            scratch=[pltpu.VMEM((piece_rows, wide), jnp.bfloat16), pltpu.VMEM((piece_rows, width), jnp.float32)],
            aliases={8: 1, 9: 2},
        )
        moving = [p for p in range(1, sections) if 0 <= step - skew * (sections - 1 - p) < pieces]
        if moving:
            back = lax.ppermute(back, axes, [(device(p, home(p)), device(p - 1, home(p - 1))) for p in moving])
        arrived.append(back)

    grads = call(
        functools.partial(weight_kernel, lines),
        "weight",
        [bf16((block + tail_rows, width))] * lines,
        [plan, layer_scale, total, act, store],
        scratch=[pltpu.VMEM((lines, block, width), jnp.bfloat16), pltpu.SemaphoreType.DMA((lines,))],
        loose=downs,
    )
    result = jnp.where(at_home, grads[0], jnp.zeros_like(grads[0]))
    for part in range(1, lines):
        result = result + from_home(grads[part], part)
    tail = result[block:].astype(jnp.float32)
    gain_total = tail[0] + tail[1] + tail[2]
    scale_total = tail[3] + tail[4] + tail[5]
    return (result[None, :block], gain_total[None], scale_total[None])


def solution(mesh):
    return jax.shard_map(
        shards,
        mesh=mesh,
        in_specs=(
            P("pipe", "dp", None),
            P("pipe", "dp", None),
            P("pipe", "dp", None),
            P("pipe", None),
            P("pipe", None),
            P("dp", None),
            P("dp", None),
        ),
        out_specs=(P("pipe", "dp", None), P("pipe", None), P("pipe", None)),
        check_vma=False,
    )
```

```python
import functools
import math

import jax
import jax.numpy as jnp
from jax import lax
from jax.experimental import pallas as pl
from jax.experimental.pallas import tpu as pltpu
from jax.sharding import PartitionSpec as P

epsilon = 1e-06
slope = math.sqrt(2.0 / math.pi)
cubic = 0.044715
NN = (((1,), (0,)), ((), ()))
TN = (((0,), (0,)), ((), ()))
axes = ("pipe", "dp")
skew = 2
in_vmem = pl.BlockSpec(memory_space=pltpu.VMEM)
anywhere = pl.BlockSpec(memory_space=pl.ANY)
in_smem = pl.BlockSpec(memory_space=pltpu.SMEM)


def held(array):
    return pltpu.with_memory_space_constraint(array, pltpu.VMEM)


def dot(a, b, dims):
    return lax.dot_general(a, b, dims, preferred_element_type=jnp.float32)


def bf16(shape):
    return jax.ShapeDtypeStruct(shape, jnp.bfloat16)


def home_of(section, lines):
    middle = lines // 2
    return middle if ((section + 1) // 2) % 2 == 0 else max(middle - 1, 0)


def span(index, size):
    return pl.ds(pl.multiple_of(index * size, size), size)


def pack_kernel(lengths_ref, x_in, start_in, up_in, out_ref, x_ref, start_ref, sems):
    batches, (row_count, width) = lengths_ref.shape[1], x_ref.shape
    depth, wide = up_in.shape
    folds = wide // width
    rows = (out_ref.shape[0] - folds * depth) // 2
    copies = [
        pltpu.make_async_copy(x_in, x_ref, sems.at[0]),
        pltpu.make_async_copy(start_in, start_ref, sems.at[1]),
    ]
    for fold in range(folds):
        source = up_in.at[:, fold * width : (fold + 1) * width]
        target = out_ref.at[pl.ds(2 * rows + fold * depth, depth)]
        copies.append(pltpu.make_async_copy(source, target, sems.at[2 + fold]))
    for copy in copies:
        copy.start()
    slot_rows = row_count // batches
    packed = lax.broadcasted_iota(jnp.int32, (rows, row_count), 0)
    source = lax.broadcasted_iota(jnp.int32, (rows, row_count), 1)
    before = jnp.int32(0)
    wanted = packed
    for m in range(batches):
        wanted = jnp.where(packed >= before, packed - before + m * slot_rows, wanted)
        before = before + lengths_ref[0, m]
    picker = jnp.where(source == wanted, 1.0, 0.0).astype(jnp.bfloat16)
    for copy in copies:
        copy.wait()
    out_ref[:rows, :] = dot(picker, x_ref[...], NN).astype(jnp.bfloat16)
    out_ref[rows : 2 * rows, :] = dot(picker, start_ref[...], NN).astype(jnp.bfloat16)


def hidden_kernel(lines, rows, plan_ref, gain_ref, *refs):
    part_refs, (act_ref, rise_ref, x_all_ref, store_ref, turned_ref, up_ref, normed_ref, sems) = refs[:lines], refs[lines:]
    width, wide = up_ref.shape
    depth, folds = width // lines, wide // width
    chunk = math.gcd(wide, 512)
    line = plan_ref[2]
    copies = []
    for part in range(lines):
        shard = lax.rem(line + part, lines)
        place, deep = span(shard, rows), span(shard, depth)
        moves = [
            (part_refs[part].at[:rows], x_all_ref.at[place]),
            (part_refs[part].at[rows : 2 * rows], store_ref.at[place]),
        ]
        for fold in range(folds):
            source = part_refs[part].at[2 * rows + fold * depth : 2 * rows + (fold + 1) * depth]
            moves.append((source, up_ref.at[deep, fold * width : (fold + 1) * width]))
        for index, (source, target) in enumerate(moves):
            copies.append(pltpu.make_async_copy(source, target, sems.at[part, index]))
    for copy in copies:
        copy.start()
    for copy in copies:
        copy.wait()

    @pl.loop(0, lines)
    def piece(index):
        place = span(index, rows)
        x = x_all_ref[place, :].astype(jnp.float32)
        inverse = lax.rsqrt(jnp.mean(x * x, axis=-1, keepdims=True) + epsilon)
        normed_ref[...] = (x * inverse * gain_ref[...]).astype(jnp.bfloat16)
        for start in range(0, wide, chunk):
            columns = slice(start, start + chunk)
            hidden = dot(normed_ref[...], up_ref[:, columns], NN)
            square = hidden * hidden
            bent = jnp.tanh(slope * hidden * (1.0 + cubic * square))
            half = 0.5 + 0.5 * bent
            act_ref[place, columns] = (hidden * half).astype(jnp.bfloat16)
            rise = half + (0.5 * slope) * hidden * (1.0 - bent * bent) * (1.0 + (3.0 * cubic) * square)
            rise_ref[place, columns] = rise.astype(jnp.bfloat16)

    turn_over(up_ref, turned_ref)


def turn_over(flat_ref, turned_ref):
    chunk = math.gcd(flat_ref.shape[1], 256)

    @pl.loop(0, flat_ref.shape[1] // chunk)
    def strip(index):
        strip = span(index, chunk)
        turned_ref[strip, :] = flat_ref[:, strip].T


def fetch(plan_ref, sources, target, sem):
    def each(act):
        for index, source in enumerate(sources):

            @pl.when(jnp.logical_or(len(sources) == 1, plan_ref[3] == index))
            def chosen():
                act(pltpu.make_async_copy(source, target, sem))

    each(lambda copy: copy.start())
    return lambda: each(lambda copy: copy.wait())


def place_kernel(part, lines, plan_ref, turned_in, *refs):
    source_refs, (turned_ref, flat_ref, sem) = refs[:-3], refs[-3:]
    block, width = flat_ref.shape
    fetch(plan_ref, source_refs, flat_ref, sem)()
    columns = span(lax.rem(plan_ref[2] + part, lines), block)
    chunk = math.gcd(width, 256)

    @pl.loop(0, width // chunk)
    def strip(index):
        strip = span(index, chunk)
        turned_ref[strip, columns] = flat_ref[:, strip].T


def chain_kernel(step, rows, plan_ref, recv_ref, gain_ref, scale_ref, x_ref, rise_ref, up_ref, down_ref, *refs):
    store_in, total_in, back_ref, store_ref, total_ref, hidden_grad_ref, normed_grad_ref = refs
    width, wide = down_ref.shape
    piece = step - plan_ref[0]

    @pl.when(jnp.logical_and(piece >= 0, piece < x_ref.shape[0] // rows))
    def active():
        place = span(piece, rows)

        @pl.when(plan_ref[1] == 0)
        def received():
            store_ref[place, :] = recv_ref[...]

        upper = store_ref[place, :].astype(jnp.float32)
        branch_grad = (upper * scale_ref[...]).astype(jnp.bfloat16)
        chunk = math.gcd(wide, 512)
        for start in range(0, wide, chunk):
            grown = dot(branch_grad, down_ref[:, start : start + chunk], NN)
            rise = rise_ref[place, start : start + chunk].astype(jnp.float32)
            hidden_grad_ref[:, start : start + chunk] = (grown * rise).astype(jnp.bfloat16)
        hidden_grad = hidden_grad_ref[...]
        chunk = math.gcd(width, 256)
        for start in range(0, width, chunk):
            normed_grad_ref[:, start : start + chunk] = dot(hidden_grad, up_ref[:, start : start + chunk], NN)
        x = x_ref[place, :].astype(jnp.float32)
        inverse = lax.rsqrt(jnp.mean(x * x, axis=-1, keepdims=True) + epsilon)
        unit = x * inverse
        normed_grad = normed_grad_ref[...]
        lean = normed_grad * unit
        total_ref[...] += jnp.sum(lean, axis=0, keepdims=True)
        mean = jnp.sum(lean * gain_ref[...], axis=-1, keepdims=True) * (1.0 / width)
        back_ref[...] = (upper + inverse * (normed_grad * gain_ref[...] - unit * mean)).astype(jnp.bfloat16)


def weight_kernel(part, lines, plan_ref, scale_ref, act_ref, store_ref, *refs):
    source_refs, (grad_ref, sum_ref, down_ref, sem) = refs[:-4], refs[-4:]
    block, width = down_ref.shape
    chunk = math.gcd(block, 128)
    shard = lax.rem(plan_ref[2] + part, lines)
    copies = fetch(plan_ref, source_refs, down_ref, sem)
    sums = jnp.zeros((1, width), jnp.float32)
    for index in range(block // chunk):
        strip = slice(index * chunk, (index + 1) * chunk)
        columns = pl.ds(pl.multiple_of(shard * block + index * chunk, chunk), chunk)
        grown = dot(act_ref[:, columns], store_ref[...], TN)
        grad_ref[strip, :] = (grown * scale_ref[...]).astype(jnp.bfloat16)
        if index == 0:
            copies()
        sums += jnp.sum(grown * down_ref[strip, :].astype(jnp.float32), axis=0, keepdims=True)
    sum_ref[...] = sums


def shards(x_saved, up_weights, down_weights, norm_gain, layer_scale, cotangent, lengths):
    sections, lines = lax.axis_size("pipe"), lax.axis_size("dp")
    section, line = lax.axis_index("pipe"), lax.axis_index("dp")
    row_count, width = cotangent.shape
    wide = up_weights.shape[2]
    block = down_weights.shape[1]
    rows = row_count * 5 // 8
    total_rows = lines * rows
    splits = 1
    piece_rows = rows // splits
    pieces = lines * splits
    steps = pieces + skew * (sections - 1)
    every = range(sections)

    def device(p, z):
        return p * lines + z

    def home(p):
        return home_of(p, lines)

    def route(p, part):
        return device(p, (home(p) + part) % lines), device(p, home(p))

    def to_home(array, after=None):
        parts = [array]
        for part in range(1, lines):
            sent = array if after is None else lax.optimization_barrier((array, after[part]))[0]
            layers = [p for p in every if after is None or part != relayed or p not in top]
            parts.append(lax.ppermute(sent, axes, [route(p, part) for p in layers]))
        return parts

    relayed = lines // 2 if sections > 2 and lines > 2 else None
    top = range(sections - 2, sections) if relayed else range(0)
    detour = sections // 2

    def from_home(array, part):
        return lax.ppermute(array, axes, [route(p, part)[::-1] for p in every])

    def call(kernel, name, outs, ins, scratch=(), aliases={}, limit=16 << 20, loose=()):
        specs = [in_smem if a.dtype == jnp.int32 else in_vmem for a in ins]
        fixed = [a if a.dtype == jnp.int32 else held(a) for a in ins]
        return pl.pallas_call(
            kernel,
            out_shape=outs,
            in_specs=specs + [anywhere] * len(loose),
            out_specs=[in_vmem] * len(outs),
            scratch_shapes=list(scratch),
            input_output_aliases=aliases,
            compiler_params=pltpu.CompilerParams(vmem_limit_bytes=limit),
            name=name,
        )(*fixed, *[pltpu.with_memory_space_constraint(a, pltpu.HBM) for a in loose])

    at_home = jnp.zeros((), jnp.bool_)
    for p in every:
        at_home = jnp.logical_or(at_home, jnp.logical_and(section == p, line == home(p)))
    begin = jnp.where(at_home, skew * (sections - 1 - section), steps)
    on_top = jnp.logical_and(at_home, section >= sections - len(top))
    plan = jnp.stack([begin, section == sections - 1, line, on_top]).astype(jnp.int32)

    (pack,) = call(
        pack_kernel,
        "pack",
        [bf16((2 * rows + up_weights.shape[1] * (wide // width), width))],
        [lengths],
        scratch=[pltpu.VMEM((row_count, width), jnp.bfloat16)] * 2 + [pltpu.SemaphoreType.DMA((2 + wide // width,))],
        loose=[x_saved[0], cotangent, up_weights[0]],
    )
    packs = to_home(pack)

    down_relay = None
    if relayed:
        out = [(route(p, relayed)[0], route(p, relayed)[0] - detour * lines) for p in top]
        on = [(source, route(p, relayed)[1]) for p, (_, source) in zip(top, out)]
        down_relay = lax.ppermute(lax.ppermute(down_weights[0], axes, out), axes, on)
    downs = to_home(down_weights[0], after=packs)

    act, rise, x_all, store, up_turned = call(
        functools.partial(hidden_kernel, lines, rows),
        "hidden",
        [bf16((total_rows, wide))] * 2 + [bf16((total_rows, width))] * 2 + [bf16((wide, width))],
        [plan, norm_gain],
        scratch=[
            pltpu.VMEM((width, wide), jnp.bfloat16),
            pltpu.VMEM((rows, width), jnp.bfloat16),
            pltpu.SemaphoreType.DMA((lines, 2 + wide // width)),
        ],
        loose=packs,
    )
    down_sources = [[down] for down in downs]
    if relayed:
        down_sources[relayed].append(down_relay)
    down_turned = jnp.zeros((width, wide), jnp.bfloat16)
    for part in range(lines):
        (down_turned,) = call(
            functools.partial(place_kernel, part, lines),
            "place",
            [bf16((width, wide))],
            [plan, down_turned],
            scratch=[pltpu.VMEM((block, width), jnp.bfloat16), pltpu.SemaphoreType.DMA],
            aliases={1: 0},
            loose=down_sources[part],
        )

    total = jnp.zeros((1, width), jnp.float32)
    arrived = [jnp.zeros((piece_rows, width), jnp.bfloat16)] * skew
    for step in range(steps):
        back, store, total = call(
            functools.partial(chain_kernel, step, piece_rows),
            "chain",
            [bf16((piece_rows, width)), bf16((total_rows, width)), jax.ShapeDtypeStruct((1, width), jnp.float32)],
            [plan, arrived.pop(0), norm_gain, layer_scale, x_all, rise, up_turned, down_turned, store, total],
            scratch=[pltpu.VMEM((piece_rows, wide), jnp.bfloat16), pltpu.VMEM((piece_rows, width), jnp.float32)],
            aliases={8: 1, 9: 2},
        )
        moving = [p for p in range(1, sections) if 0 <= step - skew * (sections - 1 - p) < pieces]
        if moving:
            back = lax.ppermute(back, axes, [(device(p, home(p)), device(p - 1, home(p - 1))) for p in moving])
        arrived.append(back)

    scale_total = jnp.zeros((1, width), jnp.float32)
    weight_total = None
    for part in sorted(range(lines), key=lambda part: -min(part, lines - part)):
        grad, scale_part = call(
            functools.partial(weight_kernel, part, lines),
            "weight",
            [bf16((block, width)), jax.ShapeDtypeStruct((1, width), jnp.float32)],
            [plan, layer_scale, act, store],
            scratch=[pltpu.VMEM((block, width), jnp.bfloat16), pltpu.SemaphoreType.DMA],
            loose=down_sources[part],
        )
        grad = from_home(grad, part) if part else jnp.where(at_home, grad, jnp.zeros_like(grad))
        weight_total = grad if weight_total is None else weight_total + grad
        scale_total = scale_total + scale_part
    sums = jnp.concatenate([total, scale_total], axis=0)
    spread = jnp.where(at_home, sums, jnp.zeros_like(sums))
    for part in range(1, lines):
        spread = spread + from_home(sums, part)
    return (weight_total[None], spread[0:1], spread[1:2])


def solution(mesh):
    return jax.shard_map(
        shards,
        mesh=mesh,
        in_specs=(
            P("pipe", "dp", None),
            P("pipe", "dp", None),
            P("pipe", "dp", None),
            P("pipe", None),
            P("pipe", None),
            P("dp", None),
            P("dp", None),
        ),
        out_specs=(P("pipe", "dp", None), P("pipe", None), P("pipe", None)),
        check_vma=False,
    )
```

```python
import functools
import math

import jax
import jax.numpy as jnp
from jax import lax
from jax.experimental import pallas as pl
from jax.experimental.pallas import tpu as pltpu
from jax.sharding import PartitionSpec as P

epsilon = 1e-06
slope = math.sqrt(2.0 / math.pi)
cubic = 0.044715
NN = (((1,), (0,)), ((), ()))
TN = (((0,), (0,)), ((), ()))
axes = ("pipe", "dp")
skew = 2
in_vmem = pl.BlockSpec(memory_space=pltpu.VMEM)
anywhere = pl.BlockSpec(memory_space=pl.ANY)
in_smem = pl.BlockSpec(memory_space=pltpu.SMEM)


def held(array):
    return pltpu.with_memory_space_constraint(array, pltpu.VMEM)


def dot(a, b, dims):
    return lax.dot_general(a, b, dims, preferred_element_type=jnp.float32)


def bf16(shape):
    return jax.ShapeDtypeStruct(shape, jnp.bfloat16)


def home_of(section, lines):
    middle = lines // 2
    return middle if ((section + 1) // 2) % 2 == 0 else max(middle - 1, 0)


def span(index, size):
    return pl.ds(pl.multiple_of(index * size, size), size)


def pack_kernel(lengths_ref, x_in, start_in, up_in, out_ref, x_ref, start_ref, sems):
    batches, (row_count, width) = lengths_ref.shape[1], x_ref.shape
    depth, wide = up_in.shape
    folds = wide // width
    rows = (out_ref.shape[0] - folds * depth) // 2
    copies = [
        pltpu.make_async_copy(x_in, x_ref, sems.at[0]),
        pltpu.make_async_copy(start_in, start_ref, sems.at[1]),
    ]
    for fold in range(folds):
        source = up_in.at[:, fold * width : (fold + 1) * width]
        target = out_ref.at[pl.ds(2 * rows + fold * depth, depth)]
        copies.append(pltpu.make_async_copy(source, target, sems.at[2 + fold]))
    for copy in copies:
        copy.start()
    slot_rows = row_count // batches
    packed = lax.broadcasted_iota(jnp.int32, (rows, row_count), 0)
    source = lax.broadcasted_iota(jnp.int32, (rows, row_count), 1)
    before = jnp.int32(0)
    wanted = packed
    for m in range(batches):
        wanted = jnp.where(packed >= before, packed - before + m * slot_rows, wanted)
        before = before + lengths_ref[0, m]
    picker = jnp.where(source == wanted, 1.0, 0.0).astype(jnp.bfloat16)
    for copy in copies:
        copy.wait()
    out_ref[:rows, :] = dot(picker, x_ref[...], NN).astype(jnp.bfloat16)
    out_ref[rows : 2 * rows, :] = dot(picker, start_ref[...], NN).astype(jnp.bfloat16)


def hidden_kernel(lines, rows, plan_ref, gain_ref, *refs):
    part_refs, (act_ref, rise_ref, x_all_ref, store_ref, turned_ref, up_ref, normed_ref, sems) = refs[:lines], refs[lines:]
    width, wide = up_ref.shape
    depth, folds = width // lines, wide // width
    chunk = math.gcd(wide, 256)
    tall = rows * math.gcd(lines, 4)
    x_copies, up_copies = [], []
    for part in range(lines):
        shard = lax.rem(plan_ref[2] + part, lines)
        place = span(shard, rows)
        source = part_refs[part]
        x_copies.append(pltpu.make_async_copy(source.at[:rows], x_all_ref.at[place], sems.at[part, 0]))
        moves = [(source.at[rows : 2 * rows], store_ref.at[place])]
        for fold in range(folds):
            strip = source.at[2 * rows + fold * depth : 2 * rows + (fold + 1) * depth]
            moves.append((strip, up_ref.at[span(shard, depth), fold * width : (fold + 1) * width]))
        up_copies += [pltpu.make_async_copy(*move, sems.at[part, 1 + index]) for index, move in enumerate(moves)]
    for copy in x_copies + up_copies:
        copy.start()
    for copy in x_copies:
        copy.wait()
    for start in range(0, lines * rows, tall):
        x = x_all_ref[start : start + tall, :].astype(jnp.float32)
        inverse = lax.rsqrt(jnp.mean(x * x, axis=-1, keepdims=True) + epsilon)
        normed_ref[start : start + tall, :] = (x * inverse * gain_ref[...]).astype(jnp.bfloat16)
    for copy in up_copies:
        copy.wait()

    @pl.loop(0, wide // chunk)
    def strip(index):
        columns = span(index, chunk)
        turned_ref[columns, :] = up_ref[:, columns].T
        for start in range(0, lines * rows, tall):
            place = slice(start, start + tall)
            hidden = dot(normed_ref[place, :], up_ref[:, columns], NN)
            square = hidden * hidden
            bent = jnp.tanh(slope * hidden * (1.0 + cubic * square))
            half = 0.5 + 0.5 * bent
            act_ref[place, columns] = (hidden * half).astype(jnp.bfloat16)
            rise = half + (0.5 * slope) * hidden * (1.0 - bent * bent) * (1.0 + (3.0 * cubic) * square)
            rise_ref[place, columns] = rise.astype(jnp.bfloat16)


def choose(plan_ref, sources, act):
    for index, source in enumerate(sources):

        @pl.when(jnp.logical_or(len(sources) == 1, plan_ref[3] == index))
        def chosen():
            act(source)


def place_kernel(parts, counts, lines, plan_ref, turned_in, *refs):
    sources, (turned_ref, flat_ref, sems) = refs[:-3], refs[-3:]
    block, width = flat_ref.shape[1:]
    chunk = math.gcd(width, 256)
    groups = [sources[sum(counts[:i]) : sum(counts[: i + 1])] for i in range(len(parts))]

    def copy(i, source):
        return pltpu.make_async_copy(source, flat_ref.at[i], sems.at[i])

    for i, group in enumerate(groups):
        choose(plan_ref, group, lambda source: copy(i, source).start())
    for i, group in enumerate(groups):
        choose(plan_ref, group, lambda source: copy(i, source).wait())
        columns = span(lax.rem(plan_ref[2] + parts[i], lines), block)

        @pl.loop(0, width // chunk)
        def strip(index):
            strip = span(index, chunk)
            turned_ref[strip, columns] = flat_ref[i, :, strip].T


def chain_kernel(step, rows, plan_ref, recv_ref, gain_ref, scale_ref, x_ref, rise_ref, up_ref, down_ref, *refs):
    store_in, total_in, back_ref, store_ref, total_ref, hidden_grad_ref, normed_grad_ref = refs
    width, wide = down_ref.shape
    piece = step - plan_ref[0]

    @pl.when(jnp.logical_and(piece >= 0, piece < x_ref.shape[0] // rows))
    def active():
        place = span(piece, rows)

        @pl.when(plan_ref[1] == 0)
        def received():
            store_ref[place, :] = recv_ref[...]

        upper = store_ref[place, :].astype(jnp.float32)
        branch_grad = (upper * scale_ref[...]).astype(jnp.bfloat16)
        chunk = math.gcd(wide, 512)
        for start in range(0, wide, chunk):
            grown = dot(branch_grad, down_ref[:, start : start + chunk], NN)
            rise = rise_ref[place, start : start + chunk].astype(jnp.float32)
            hidden_grad_ref[:, start : start + chunk] = (grown * rise).astype(jnp.bfloat16)
        hidden_grad = hidden_grad_ref[...]
        chunk = math.gcd(width, 256)
        for start in range(0, width, chunk):
            normed_grad_ref[:, start : start + chunk] = dot(hidden_grad, up_ref[:, start : start + chunk], NN)
        x = x_ref[place, :].astype(jnp.float32)
        inverse = lax.rsqrt(jnp.mean(x * x, axis=-1, keepdims=True) + epsilon)
        unit = x * inverse
        normed_grad = normed_grad_ref[...]
        lean = normed_grad * unit
        total_ref[...] += jnp.sum(lean, axis=0, keepdims=True)
        mean = jnp.sum(lean * gain_ref[...], axis=-1, keepdims=True) * (1.0 / width)
        back_ref[...] = (upper + inverse * (normed_grad * gain_ref[...] - unit * mean)).astype(jnp.bfloat16)


def weight_kernel(part, lines, plan_ref, scale_ref, act_ref, store_ref, *refs):
    sources, (grad_ref, sum_ref, down_ref, sem) = refs[:-4], refs[-4:]
    block, width = down_ref.shape
    chunk = math.gcd(block, 128)
    shard = lax.rem(plan_ref[2] + part, lines)
    choose(plan_ref, sources, lambda source: pltpu.make_async_copy(source, down_ref, sem).start())
    sums = jnp.zeros((1, width), jnp.float32)
    for index in range(block // chunk):
        strip = slice(index * chunk, (index + 1) * chunk)
        columns = pl.ds(pl.multiple_of(shard * block + index * chunk, chunk), chunk)
        grown = dot(act_ref[:, columns], store_ref[...], TN)
        grad_ref[strip, :] = (grown * scale_ref[...]).astype(jnp.bfloat16)
        if index == 0:
            choose(plan_ref, sources, lambda source: pltpu.make_async_copy(source, down_ref, sem).wait())
        sums += jnp.sum(grown * down_ref[strip, :].astype(jnp.float32), axis=0, keepdims=True)
    sum_ref[...] = sums


def shards(x_saved, up_weights, down_weights, norm_gain, layer_scale, cotangent, lengths):
    sections, lines = lax.axis_size("pipe"), lax.axis_size("dp")
    section, line = lax.axis_index("pipe"), lax.axis_index("dp")
    row_count, width = cotangent.shape
    wide = up_weights.shape[2]
    block = down_weights.shape[1]
    rows = row_count * 5 // 8
    total_rows = lines * rows
    splits = 1
    piece_rows = rows // splits
    pieces = lines * splits
    steps = pieces + skew * (sections - 1)
    every = range(sections)

    def device(p, z):
        return p * lines + z

    def home(p):
        return home_of(p, lines)

    def route(p, part):
        return device(p, (home(p) + part) % lines), device(p, home(p))

    def to_home(array, after=None):
        parts = [array]
        for part in range(1, lines):
            sent = array if after is None else lax.optimization_barrier((array, after[part]))[0]
            layers = [p for p in every if after is None or part != relayed or p not in top]
            parts.append(lax.ppermute(sent, axes, [route(p, part) for p in layers]))
        return parts

    relayed = lines // 2 if sections > 2 and lines > 2 else None
    top = range(sections - 2, sections) if relayed else range(0)
    detour = sections // 2

    def from_home(array, part):
        return lax.ppermute(array, axes, [route(p, part)[::-1] for p in every])

    def call(kernel, name, outs, ins, scratch=(), aliases={}, limit=16 << 20, loose=()):
        specs = [in_smem if a.dtype == jnp.int32 else in_vmem for a in ins]
        fixed = [a if a.dtype == jnp.int32 else held(a) for a in ins]
        return pl.pallas_call(
            kernel,
            out_shape=outs,
            in_specs=specs + [anywhere] * len(loose),
            out_specs=[in_vmem] * len(outs),
            scratch_shapes=list(scratch),
            input_output_aliases=aliases,
            compiler_params=pltpu.CompilerParams(vmem_limit_bytes=limit),
            name=name,
        )(*fixed, *[pltpu.with_memory_space_constraint(a, pltpu.HBM) for a in loose])

    at_home = jnp.zeros((), jnp.bool_)
    for p in every:
        at_home = jnp.logical_or(at_home, jnp.logical_and(section == p, line == home(p)))
    begin = jnp.where(at_home, skew * (sections - 1 - section), steps)
    on_top = jnp.logical_and(at_home, section >= sections - len(top))
    plan = jnp.stack([begin, section == sections - 1, line, on_top]).astype(jnp.int32)

    (pack,) = call(
        pack_kernel,
        "pack",
        [bf16((2 * rows + up_weights.shape[1] * (wide // width), width))],
        [lengths],
        scratch=[pltpu.VMEM((row_count, width), jnp.bfloat16)] * 2 + [pltpu.SemaphoreType.DMA((2 + wide // width,))],
        loose=[x_saved[0], cotangent, up_weights[0]],
    )
    packs = to_home(pack)

    def placed(parts, turned):
        (turned,) = call(
            functools.partial(place_kernel, parts, [len(down_sources[part]) for part in parts], lines),
            "place",
            [bf16((width, wide))],
            [plan, turned],
            scratch=[pltpu.VMEM((len(parts), block, width), jnp.bfloat16), pltpu.SemaphoreType.DMA((len(parts),))],
            aliases={1: 0},
            loose=[source for part in parts for source in down_sources[part]],
        )
        return turned

    down_sources = [[down_weights[0]]]
    down_turned = placed([0], jnp.zeros((width, wide), jnp.bfloat16))
    down_relay = None
    if relayed:
        out = [(route(p, relayed)[0], route(p, relayed)[0] - detour * lines) for p in top]
        on = [(source, route(p, relayed)[1]) for p, (_, source) in zip(top, out)]
        down_relay = lax.ppermute(down_weights[0], axes, out)
        down_relay = lax.ppermute(down_relay, axes, on)
    down_sources += [[down] for down in to_home(down_weights[0], after=packs)[1:]]
    if relayed:
        down_sources[relayed].append(down_relay)

    act, rise, x_all, store, up_turned = call(
        functools.partial(hidden_kernel, lines, rows),
        "hidden",
        [bf16((total_rows, wide))] * 2 + [bf16((total_rows, width))] * 2 + [bf16((wide, width))],
        [plan, norm_gain],
        scratch=[
            pltpu.VMEM((width, wide), jnp.bfloat16),
            pltpu.VMEM((total_rows, width), jnp.bfloat16),
            pltpu.SemaphoreType.DMA((lines, 2 + wide // width)),
        ],
        loose=packs,
    )
    for index in range(1, lines, 3):
        down_turned = placed(list(range(index, min(index + 3, lines))), down_turned)

    total = jnp.zeros((1, width), jnp.float32)
    arrived = [jnp.zeros((piece_rows, width), jnp.bfloat16)] * skew
    for step in range(steps):
        back, store, total = call(
            functools.partial(chain_kernel, step, piece_rows),
            "chain",
            [bf16((piece_rows, width)), bf16((total_rows, width)), jax.ShapeDtypeStruct((1, width), jnp.float32)],
            [plan, arrived.pop(0), norm_gain, layer_scale, x_all, rise, up_turned, down_turned, store, total],
            scratch=[pltpu.VMEM((piece_rows, wide), jnp.bfloat16), pltpu.VMEM((piece_rows, width), jnp.float32)],
            aliases={8: 1, 9: 2},
        )
        moving = [p for p in range(1, sections) if 0 <= step - skew * (sections - 1 - p) < pieces]
        if moving:
            back = lax.ppermute(back, axes, [(device(p, home(p)), device(p - 1, home(p - 1))) for p in moving])
        arrived.append(back)

    scale_total = jnp.zeros((1, width), jnp.float32)
    weight_total = None
    for part in sorted(range(lines), key=lambda part: -min(part, lines - part)):
        grad, scale_part = call(
            functools.partial(weight_kernel, part, lines),
            "weight",
            [bf16((block, width)), jax.ShapeDtypeStruct((1, width), jnp.float32)],
            [plan, layer_scale, act, store],
            scratch=[pltpu.VMEM((block, width), jnp.bfloat16), pltpu.SemaphoreType.DMA],
            loose=down_sources[part],
        )
        grad = from_home(grad, part) if part else jnp.where(at_home, grad, jnp.zeros_like(grad))
        weight_total = grad if weight_total is None else weight_total + grad
        scale_total = scale_total + scale_part
    sums = jnp.concatenate([total, scale_total], axis=0)
    spread = jnp.where(at_home, sums, jnp.zeros_like(sums))
    for part in range(1, lines):
        spread = spread + from_home(sums, part)
    return (weight_total[None], spread[0:1], spread[1:2])


def solution(mesh):
    return jax.shard_map(
        shards,
        mesh=mesh,
        in_specs=(
            P("pipe", "dp", None),
            P("pipe", "dp", None),
            P("pipe", "dp", None),
            P("pipe", None),
            P("pipe", None),
            P("dp", None),
            P("dp", None),
        ),
        out_specs=(P("pipe", "dp", None), P("pipe", None), P("pipe", None)),
        check_vma=False,
    )
```

```python
import functools
import math

import jax
import jax.numpy as jnp
from jax import lax
from jax.experimental import pallas as pl
from jax.experimental.pallas import tpu as pltpu
from jax.sharding import PartitionSpec as P

epsilon = 1e-06
slope = math.sqrt(2.0 / math.pi)
cubic = 0.044715
NN = (((1,), (0,)), ((), ()))
TN = (((0,), (0,)), ((), ()))
axes = ("pipe", "dp")
skew = 2
in_vmem = pl.BlockSpec(memory_space=pltpu.VMEM)
anywhere = pl.BlockSpec(memory_space=pl.ANY)
in_smem = pl.BlockSpec(memory_space=pltpu.SMEM)


def held(array):
    return pltpu.with_memory_space_constraint(array, pltpu.VMEM)


def dot(a, b, dims):
    return lax.dot_general(a, b, dims, preferred_element_type=jnp.float32)


def bf16(shape):
    return jax.ShapeDtypeStruct(shape, jnp.bfloat16)


def home_of(section, lines):
    middle = lines // 2
    return middle if ((section + 1) // 2) % 2 == 0 else max(middle - 1, 0)


def span(index, size):
    return pl.ds(pl.multiple_of(index * size, size), size)


def pack_kernel(lengths_ref, x_in, start_in, up_in, out_ref, x_ref, start_ref, sems):
    batches, (row_count, width) = lengths_ref.shape[1], x_ref.shape
    depth, wide = up_in.shape
    folds = wide // width
    rows = (out_ref.shape[0] - folds * depth) // 2
    copies = [
        pltpu.make_async_copy(x_in, x_ref, sems.at[0]),
        pltpu.make_async_copy(start_in, start_ref, sems.at[1]),
    ]
    for fold in range(folds):
        source = up_in.at[:, fold * width : (fold + 1) * width]
        target = out_ref.at[pl.ds(2 * rows + fold * depth, depth)]
        copies.append(pltpu.make_async_copy(source, target, sems.at[2 + fold]))
    for copy in copies:
        copy.start()
    slot_rows = row_count // batches
    packed = lax.broadcasted_iota(jnp.int32, (rows, row_count), 0)
    source = lax.broadcasted_iota(jnp.int32, (rows, row_count), 1)
    before = jnp.int32(0)
    wanted = packed
    for m in range(batches):
        wanted = jnp.where(packed >= before, packed - before + m * slot_rows, wanted)
        before = before + lengths_ref[0, m]
    picker = jnp.where(source == wanted, 1.0, 0.0).astype(jnp.bfloat16)
    for copy in copies:
        copy.wait()
    out_ref[:rows, :] = dot(picker, x_ref[...], NN).astype(jnp.bfloat16)
    out_ref[rows : 2 * rows, :] = dot(picker, start_ref[...], NN).astype(jnp.bfloat16)


def hidden_kernel(lines, rows, plan_ref, gain_ref, *refs):
    part_refs, (act_ref, rise_ref, x_all_ref, store_ref, turned_ref, up_ref, normed_ref, sems) = refs[:lines], refs[lines:]
    width, wide = up_ref.shape
    depth, folds = width // lines, wide // width
    chunk = math.gcd(wide, 256)
    tall = rows * math.gcd(lines, 4)
    x_copies, up_copies = [], []
    for part in range(lines):
        shard = lax.rem(plan_ref[2] + part, lines)
        place = span(shard, rows)
        source = part_refs[part]
        x_copies.append(pltpu.make_async_copy(source.at[:rows], x_all_ref.at[place], sems.at[part, 0]))
        moves = [(source.at[rows : 2 * rows], store_ref.at[place])]
        for fold in range(folds):
            strip = source.at[2 * rows + fold * depth : 2 * rows + (fold + 1) * depth]
            moves.append((strip, up_ref.at[span(shard, depth), fold * width : (fold + 1) * width]))
        up_copies += [pltpu.make_async_copy(*move, sems.at[part, 1 + index]) for index, move in enumerate(moves)]
    for copy in x_copies + up_copies:
        copy.start()
    for copy in x_copies:
        copy.wait()
    for start in range(0, lines * rows, tall):
        x = x_all_ref[start : start + tall, :].astype(jnp.float32)
        inverse = lax.rsqrt(jnp.mean(x * x, axis=-1, keepdims=True) + epsilon)
        normed_ref[start : start + tall, :] = (x * inverse * gain_ref[...]).astype(jnp.bfloat16)
    for copy in up_copies:
        copy.wait()

    @pl.loop(0, wide // chunk)
    def strip(index):
        columns = span(index, chunk)
        turned_ref[columns, :] = up_ref[:, columns].T
        for start in range(0, lines * rows, tall):
            place = slice(start, start + tall)
            hidden = dot(normed_ref[place, :], up_ref[:, columns], NN)
            square = hidden * hidden
            bent = jnp.tanh(slope * hidden * (1.0 + cubic * square))
            half = 0.5 + 0.5 * bent
            act_ref[place, columns] = (hidden * half).astype(jnp.bfloat16)
            rise = half + (0.5 * slope) * hidden * (1.0 - bent * bent) * (1.0 + (3.0 * cubic) * square)
            rise_ref[place, columns] = rise.astype(jnp.bfloat16)


def choose(plan_ref, sources, act):
    for index, source in enumerate(sources):

        @pl.when(jnp.logical_or(len(sources) == 1, plan_ref[3] == index))
        def chosen():
            act(source)


def place_kernel(parts, counts, lines, plan_ref, turned_in, *refs):
    sources, (turned_ref, flat_ref, sems) = refs[:-3], refs[-3:]
    block, width = flat_ref.shape[1:]
    chunk = math.gcd(width, 256)
    groups = [sources[sum(counts[:i]) : sum(counts[: i + 1])] for i in range(len(parts))]

    def copy(i, source):
        return pltpu.make_async_copy(source, flat_ref.at[i], sems.at[i])

    for i, group in enumerate(groups):
        choose(plan_ref, group, lambda source: copy(i, source).start())
    for i, group in enumerate(groups):
        choose(plan_ref, group, lambda source: copy(i, source).wait())
        columns = span(lax.rem(plan_ref[2] + parts[i], lines), block)

        @pl.loop(0, width // chunk)
        def strip(index):
            strip = span(index, chunk)
            turned_ref[strip, columns] = flat_ref[i, :, strip].T


def chain_kernel(step, rows, plan_ref, recv_ref, gain_ref, scale_ref, x_ref, rise_ref, up_ref, down_ref, *refs):
    store_in, total_in, back_ref, store_ref, total_ref, hidden_grad_ref, normed_grad_ref = refs
    width, wide = down_ref.shape
    piece = step - plan_ref[0]

    @pl.when(jnp.logical_and(piece >= 0, piece < x_ref.shape[0] // rows))
    def active():
        place = span(piece, rows)

        @pl.when(plan_ref[1] == 0)
        def received():
            store_ref[place, :] = recv_ref[...]

        upper = store_ref[place, :].astype(jnp.float32)
        branch_grad = (upper * scale_ref[...]).astype(jnp.bfloat16)
        chunk = math.gcd(wide, 512)
        for start in range(0, wide, chunk):
            grown = dot(branch_grad, down_ref[:, start : start + chunk], NN)
            rise = rise_ref[place, start : start + chunk].astype(jnp.float32)
            hidden_grad_ref[:, start : start + chunk] = (grown * rise).astype(jnp.bfloat16)
        hidden_grad = hidden_grad_ref[...]
        chunk = math.gcd(width, 256)
        for start in range(0, width, chunk):
            normed_grad_ref[:, start : start + chunk] = dot(hidden_grad, up_ref[:, start : start + chunk], NN)
        x = x_ref[place, :].astype(jnp.float32)
        inverse = lax.rsqrt(jnp.mean(x * x, axis=-1, keepdims=True) + epsilon)
        unit = x * inverse
        normed_grad = normed_grad_ref[...]
        lean = normed_grad * unit
        total_ref[...] += jnp.sum(lean, axis=0, keepdims=True)
        mean = jnp.sum(lean * gain_ref[...], axis=-1, keepdims=True) * (1.0 / width)
        back_ref[...] = (upper + inverse * (normed_grad * gain_ref[...] - unit * mean)).astype(jnp.bfloat16)


def weight_kernel(part, lines, plan_ref, scale_ref, act_ref, store_ref, *refs):
    sources, (grad_ref, sum_ref, down_ref, sem) = refs[:-4], refs[-4:]
    block, width = down_ref.shape
    chunk = math.gcd(block, 128)
    shard = lax.rem(plan_ref[2] + part, lines)
    choose(plan_ref, sources, lambda source: pltpu.make_async_copy(source, down_ref, sem).start())
    sums = jnp.zeros((1, width), jnp.float32)
    for index in range(block // chunk):
        strip = slice(index * chunk, (index + 1) * chunk)
        columns = pl.ds(pl.multiple_of(shard * block + index * chunk, chunk), chunk)
        grown = dot(act_ref[:, columns], store_ref[...], TN)
        grad_ref[strip, :] = (grown * scale_ref[...]).astype(jnp.bfloat16)
        if index == 0:
            choose(plan_ref, sources, lambda source: pltpu.make_async_copy(source, down_ref, sem).wait())
        sums += jnp.sum(grown * down_ref[strip, :].astype(jnp.float32), axis=0, keepdims=True)
    sum_ref[...] = sums


def shards(x_saved, up_weights, down_weights, norm_gain, layer_scale, cotangent, lengths):
    sections, lines = lax.axis_size("pipe"), lax.axis_size("dp")
    section, line = lax.axis_index("pipe"), lax.axis_index("dp")
    row_count, width = cotangent.shape
    wide = up_weights.shape[2]
    block = down_weights.shape[1]
    rows = row_count * 5 // 8
    total_rows = lines * rows
    piece_rows = 128 if total_rows % 128 == 0 else rows
    pieces = total_rows // piece_rows
    steps = pieces + skew * (sections - 1)
    every = range(sections)

    def device(p, z):
        return p * lines + z

    def home(p):
        return home_of(p, lines)

    def route(p, part):
        return device(p, (home(p) + part) % lines), device(p, home(p))

    def to_home(array, after=None):
        parts = [array]
        for part in range(1, lines):
            sent = array if after is None else lax.optimization_barrier((array, after[1]))[0]
            layers = [p for p in every if after is None or part != relayed or p not in top]
            parts.append(lax.ppermute(sent, axes, [route(p, part) for p in layers]))
        return parts

    relayed = lines // 2 if sections > 2 and lines > 2 else None
    top = range(sections - 2, sections) if relayed else range(0)
    detour = sections // 2

    def from_home(array, part):
        return lax.ppermute(array, axes, [route(p, part)[::-1] for p in every])

    def call(kernel, name, outs, ins, scratch=(), aliases={}, limit=16 << 20, loose=()):
        specs = [in_smem if a.dtype == jnp.int32 else in_vmem for a in ins]
        fixed = [a if a.dtype == jnp.int32 else held(a) for a in ins]
        return pl.pallas_call(
            kernel,
            out_shape=outs,
            in_specs=specs + [anywhere] * len(loose),
            out_specs=[in_vmem] * len(outs),
            scratch_shapes=list(scratch),
            input_output_aliases=aliases,
            compiler_params=pltpu.CompilerParams(vmem_limit_bytes=limit),
            name=name,
        )(*fixed, *[pltpu.with_memory_space_constraint(a, pltpu.HBM) for a in loose])

    at_home = jnp.zeros((), jnp.bool_)
    for p in every:
        at_home = jnp.logical_or(at_home, jnp.logical_and(section == p, line == home(p)))
    begin = jnp.where(at_home, skew * (sections - 1 - section), steps)
    on_top = jnp.logical_and(at_home, section >= sections - len(top))
    plan = jnp.stack([begin, section == sections - 1, line, on_top]).astype(jnp.int32)

    (pack,) = call(
        pack_kernel,
        "pack",
        [bf16((2 * rows + up_weights.shape[1] * (wide // width), width))],
        [lengths],
        scratch=[pltpu.VMEM((row_count, width), jnp.bfloat16)] * 2 + [pltpu.SemaphoreType.DMA((2 + wide // width,))],
        loose=[x_saved[0], cotangent, up_weights[0]],
    )
    packs = to_home(pack)

    def placed(parts, turned):
        (turned,) = call(
            functools.partial(place_kernel, parts, [len(down_sources[part]) for part in parts], lines),
            "place",
            [bf16((width, wide))],
            [plan, turned],
            scratch=[pltpu.VMEM((len(parts), block, width), jnp.bfloat16), pltpu.SemaphoreType.DMA((len(parts),))],
            aliases={1: 0},
            loose=[source for part in parts for source in down_sources[part]],
        )
        return turned

    down_sources = [[down_weights[0]]]
    down_turned = placed([0], jnp.zeros((width, wide), jnp.bfloat16))
    down_relay = None
    if relayed:
        out = [(route(p, relayed)[0], route(p, relayed)[0] - detour * lines) for p in top]
        on = [(source, route(p, relayed)[1]) for p, (_, source) in zip(top, out)]
        down_relay = lax.ppermute(down_weights[0], axes, out)
        down_relay = lax.ppermute(down_relay, axes, on)
    down_sources += [[down] for down in to_home(down_weights[0], after=packs)[1:]]
    if relayed:
        down_sources[relayed].append(down_relay)

    act, rise, x_all, store, up_turned = call(
        functools.partial(hidden_kernel, lines, rows),
        "hidden",
        [bf16((total_rows, wide))] * 2 + [bf16((total_rows, width))] * 2 + [bf16((wide, width))],
        [plan, norm_gain],
        scratch=[
            pltpu.VMEM((width, wide), jnp.bfloat16),
            pltpu.VMEM((total_rows, width), jnp.bfloat16),
            pltpu.SemaphoreType.DMA((lines, 2 + wide // width)),
        ],
        loose=packs,
    )
    for index in range(1, lines, 3):
        down_turned = placed(list(range(index, min(index + 3, lines))), down_turned)

    total = jnp.zeros((1, width), jnp.float32)
    arrived = [jnp.zeros((piece_rows, width), jnp.bfloat16)] * skew
    for step in range(steps):
        back, store, total = call(
            functools.partial(chain_kernel, step, piece_rows),
            "chain",
            [bf16((piece_rows, width)), bf16((total_rows, width)), jax.ShapeDtypeStruct((1, width), jnp.float32)],
            [plan, arrived.pop(0), norm_gain, layer_scale, x_all, rise, up_turned, down_turned, store, total],
            scratch=[pltpu.VMEM((piece_rows, wide), jnp.bfloat16), pltpu.VMEM((piece_rows, width), jnp.float32)],
            aliases={8: 1, 9: 2},
        )
        moving = [p for p in range(1, sections) if 0 <= step - skew * (sections - 1 - p) < pieces]
        if moving:
            back = lax.ppermute(back, axes, [(device(p, home(p)), device(p - 1, home(p - 1))) for p in moving])
        arrived.append(back)

    scale_total = jnp.zeros((1, width), jnp.float32)
    weight_total = None
    for part in sorted(range(lines), key=lambda part: -min(part, lines - part)):
        grad, scale_part = call(
            functools.partial(weight_kernel, part, lines),
            "weight",
            [bf16((block, width)), jax.ShapeDtypeStruct((1, width), jnp.float32)],
            [plan, layer_scale, act, store],
            scratch=[pltpu.VMEM((block, width), jnp.bfloat16), pltpu.SemaphoreType.DMA],
            loose=down_sources[part],
        )
        grad = from_home(grad, part) if part else jnp.where(at_home, grad, jnp.zeros_like(grad))
        weight_total = grad if weight_total is None else weight_total + grad
        scale_total = scale_total + scale_part
    sums = jnp.concatenate([total, scale_total], axis=0)
    spread = jnp.where(at_home, sums, jnp.zeros_like(sums))
    for part in range(1, lines):
        spread = spread + from_home(sums, part)
    return (weight_total[None], spread[0:1], spread[1:2])


def solution(mesh):
    return jax.shard_map(
        shards,
        mesh=mesh,
        in_specs=(
            P("pipe", "dp", None),
            P("pipe", "dp", None),
            P("pipe", "dp", None),
            P("pipe", None),
            P("pipe", None),
            P("dp", None),
            P("dp", None),
        ),
        out_specs=(P("pipe", "dp", None), P("pipe", None), P("pipe", None)),
        check_vma=False,
    )
```

```python
import functools
import math

import jax
import jax.numpy as jnp
from jax import lax
from jax.experimental import pallas as pl
from jax.experimental.pallas import tpu as pltpu
from jax.sharding import PartitionSpec as P

epsilon = 1e-06
slope = math.sqrt(2.0 / math.pi)
cubic = 0.044715
NN = (((1,), (0,)), ((), ()))
TN = (((0,), (0,)), ((), ()))
axes = ("pipe", "dp")
skew = 2
in_vmem = pl.BlockSpec(memory_space=pltpu.VMEM)
anywhere = pl.BlockSpec(memory_space=pl.ANY)
in_smem = pl.BlockSpec(memory_space=pltpu.SMEM)


def held(array):
    return pltpu.with_memory_space_constraint(array, pltpu.VMEM)


def dot(a, b, dims):
    return lax.dot_general(a, b, dims, preferred_element_type=jnp.float32)


def bf16(shape):
    return jax.ShapeDtypeStruct(shape, jnp.bfloat16)


def home_of(section, lines):
    middle = lines // 2
    return middle if ((section + 1) // 2) % 2 == 0 else max(middle - 1, 0)


def span(index, size):
    return pl.ds(pl.multiple_of(index * size, size), size)


def pack_kernel(lengths_ref, x_in, start_in, up_in, out_ref, x_ref, start_ref, sems):
    batches, (row_count, width) = lengths_ref.shape[1], x_ref.shape
    depth, wide = up_in.shape
    folds = wide // width
    rows = (out_ref.shape[0] - folds * depth) // 2
    copies = [
        pltpu.make_async_copy(x_in, x_ref, sems.at[0]),
        pltpu.make_async_copy(start_in, start_ref, sems.at[1]),
    ]
    for fold in range(folds):
        source = up_in.at[:, fold * width : (fold + 1) * width]
        target = out_ref.at[pl.ds(2 * rows + fold * depth, depth)]
        copies.append(pltpu.make_async_copy(source, target, sems.at[2 + fold]))
    for copy in copies:
        copy.start()
    slot_rows = row_count // batches
    packed = lax.broadcasted_iota(jnp.int32, (rows, row_count), 0)
    source = lax.broadcasted_iota(jnp.int32, (rows, row_count), 1)
    before = jnp.int32(0)
    wanted = packed
    for m in range(batches):
        wanted = jnp.where(packed >= before, packed - before + m * slot_rows, wanted)
        before = before + lengths_ref[0, m]
    picker = jnp.where(source == wanted, 1.0, 0.0).astype(jnp.bfloat16)
    for copy in copies:
        copy.wait()
    out_ref[:rows, :] = dot(picker, x_ref[...], NN).astype(jnp.bfloat16)
    out_ref[rows : 2 * rows, :] = dot(picker, start_ref[...], NN).astype(jnp.bfloat16)


def hidden_kernel(lines, rows, plan_ref, gain_ref, *refs):
    part_refs, (act_ref, rise_ref, x_all_ref, store_ref, turned_ref, up_ref, normed_ref, sems) = refs[:lines], refs[lines:]
    width, wide = up_ref.shape
    depth, folds = width // lines, wide // width
    chunk = math.gcd(wide, 256)
    tall = rows * math.gcd(lines, 4)
    x_copies, up_copies = [], []
    for part in range(lines):
        shard = lax.rem(plan_ref[2] + part, lines)
        place = span(shard, rows)
        source = part_refs[part]
        x_copies.append(pltpu.make_async_copy(source.at[:rows], x_all_ref.at[place], sems.at[part, 0]))
        moves = [(source.at[rows : 2 * rows], store_ref.at[place])]
        for fold in range(folds):
            strip = source.at[2 * rows + fold * depth : 2 * rows + (fold + 1) * depth]
            moves.append((strip, up_ref.at[span(shard, depth), fold * width : (fold + 1) * width]))
        up_copies += [pltpu.make_async_copy(*move, sems.at[part, 1 + index]) for index, move in enumerate(moves)]
    for copy in x_copies + up_copies:
        copy.start()
    for copy in x_copies:
        copy.wait()
    for start in range(0, lines * rows, tall):
        x = x_all_ref[start : start + tall, :].astype(jnp.float32)
        inverse = lax.rsqrt(jnp.mean(x * x, axis=-1, keepdims=True) + epsilon)
        normed_ref[start : start + tall, :] = (x * inverse * gain_ref[...]).astype(jnp.bfloat16)
    for copy in up_copies:
        copy.wait()

    @pl.loop(0, wide // chunk)
    def strip(index):
        columns = span(index, chunk)
        turned_ref[columns, :] = up_ref[:, columns].T
        for start in range(0, lines * rows, tall):
            place = slice(start, start + tall)
            hidden = dot(normed_ref[place, :], up_ref[:, columns], NN)
            square = hidden * hidden
            bent = jnp.tanh(slope * hidden * (1.0 + cubic * square))
            half = 0.5 + 0.5 * bent
            act_ref[place, columns] = (hidden * half).astype(jnp.bfloat16)
            rise = half + (0.5 * slope) * hidden * (1.0 - bent * bent) * (1.0 + (3.0 * cubic) * square)
            rise_ref[place, columns] = rise.astype(jnp.bfloat16)


def choose(plan_ref, sources, act):
    for index, source in enumerate(sources):

        @pl.when(jnp.logical_or(len(sources) == 1, plan_ref[3] == index))
        def chosen():
            act(source)


def place_kernel(parts, counts, lines, plan_ref, turned_in, *refs):
    sources, (turned_ref, flat_ref, sems) = refs[:-3], refs[-3:]
    block, width = flat_ref.shape[1:]
    chunk = math.gcd(width, 256)
    groups = [sources[sum(counts[:i]) : sum(counts[: i + 1])] for i in range(len(parts))]

    def copy(i, source):
        return pltpu.make_async_copy(source, flat_ref.at[i], sems.at[i])

    for i, group in enumerate(groups):
        choose(plan_ref, group, lambda source: copy(i, source).start())
    for i, group in enumerate(groups):
        choose(plan_ref, group, lambda source: copy(i, source).wait())
        columns = span(lax.rem(plan_ref[2] + parts[i], lines), block)

        @pl.loop(0, width // chunk)
        def strip(index):
            strip = span(index, chunk)
            turned_ref[strip, columns] = flat_ref[i, :, strip].T


def chain_kernel(step, rows, plan_ref, recv_ref, gain_ref, scale_ref, x_ref, rise_ref, up_ref, down_ref, *refs):
    store_in, total_in, back_ref, store_ref, total_ref, hidden_grad_ref, normed_grad_ref = refs
    width, wide = down_ref.shape
    piece = step - plan_ref[0]

    @pl.when(jnp.logical_and(piece >= 0, piece < x_ref.shape[0] // rows))
    def active():
        place = span(piece, rows)

        @pl.when(plan_ref[1] == 0)
        def received():
            store_ref[place, :] = recv_ref[...]

        upper = store_ref[place, :].astype(jnp.float32)
        branch_grad = (upper * scale_ref[...]).astype(jnp.bfloat16)
        chunk = math.gcd(wide, 512)
        for start in range(0, wide, chunk):
            grown = dot(branch_grad, down_ref[:, start : start + chunk], NN)
            rise = rise_ref[place, start : start + chunk].astype(jnp.float32)
            hidden_grad_ref[:, start : start + chunk] = (grown * rise).astype(jnp.bfloat16)
        hidden_grad = hidden_grad_ref[...]
        chunk = math.gcd(width, 256)
        for start in range(0, width, chunk):
            normed_grad_ref[:, start : start + chunk] = dot(hidden_grad, up_ref[:, start : start + chunk], NN)
        x = x_ref[place, :].astype(jnp.float32)
        inverse = lax.rsqrt(jnp.mean(x * x, axis=-1, keepdims=True) + epsilon)
        unit = x * inverse
        normed_grad = normed_grad_ref[...]
        lean = normed_grad * unit
        total_ref[...] += jnp.sum(lean, axis=0, keepdims=True)
        mean = jnp.sum(lean * gain_ref[...], axis=-1, keepdims=True) * (1.0 / width)
        back_ref[...] = (upper + inverse * (normed_grad * gain_ref[...] - unit * mean)).astype(jnp.bfloat16)


def weight_kernel(part, lines, plan_ref, scale_ref, act_ref, store_ref, *refs):
    sources, (grad_ref, sum_ref, down_ref, sem) = refs[:-4], refs[-4:]
    block, width = down_ref.shape
    chunk = math.gcd(block, 256)
    shard = lax.rem(plan_ref[2] + part, lines)
    choose(plan_ref, sources, lambda source: pltpu.make_async_copy(source, down_ref, sem).start())
    choose(plan_ref, sources, lambda source: pltpu.make_async_copy(source, down_ref, sem).wait())
    sum_ref[...] = jnp.zeros((1, width), jnp.float32)

    @pl.loop(0, block // chunk)
    def strip(index):
        strip = span(index, chunk)
        columns = pl.ds(pl.multiple_of(shard * block + index * chunk, chunk), chunk)
        grown = dot(act_ref[:, columns], store_ref[...], TN)
        grad_ref[strip, :] = (grown * scale_ref[...]).astype(jnp.bfloat16)
        sum_ref[...] += jnp.sum(grown * down_ref[strip, :].astype(jnp.float32), axis=0, keepdims=True)


def shards(x_saved, up_weights, down_weights, norm_gain, layer_scale, cotangent, lengths):
    sections, lines = lax.axis_size("pipe"), lax.axis_size("dp")
    section, line = lax.axis_index("pipe"), lax.axis_index("dp")
    row_count, width = cotangent.shape
    wide = up_weights.shape[2]
    block = down_weights.shape[1]
    rows = row_count * 5 // 8
    total_rows = lines * rows
    piece_rows = 128 if total_rows % 128 == 0 else rows
    pieces = total_rows // piece_rows
    steps = pieces + skew * (sections - 1)
    every = range(sections)

    def device(p, z):
        return p * lines + z

    def home(p):
        return home_of(p, lines)

    def route(p, part):
        return device(p, (home(p) + part) % lines), device(p, home(p))

    def to_home(array, after=None):
        parts = [array]
        for part in range(1, lines):
            sent = array if after is None else lax.optimization_barrier((array, after[1]))[0]
            layers = [p for p in every if after is None or part != relayed or p not in top]
            parts.append(lax.ppermute(sent, axes, [route(p, part) for p in layers]))
        return parts

    relayed = lines // 2 if sections > 2 and lines > 2 else None
    top = range(sections - 2, sections) if relayed else range(0)
    detour = sections // 2

    def from_home(array, part):
        return lax.ppermute(array, axes, [route(p, part)[::-1] for p in every])

    def call(kernel, name, outs, ins, scratch=(), aliases={}, limit=16 << 20, loose=()):
        specs = [in_smem if a.dtype == jnp.int32 else in_vmem for a in ins]
        fixed = [a if a.dtype == jnp.int32 else held(a) for a in ins]
        return pl.pallas_call(
            kernel,
            out_shape=outs,
            in_specs=specs + [anywhere] * len(loose),
            out_specs=[in_vmem] * len(outs),
            scratch_shapes=list(scratch),
            input_output_aliases=aliases,
            compiler_params=pltpu.CompilerParams(vmem_limit_bytes=limit),
            name=name,
        )(*fixed, *[pltpu.with_memory_space_constraint(a, pltpu.HBM) for a in loose])

    at_home = jnp.zeros((), jnp.bool_)
    for p in every:
        at_home = jnp.logical_or(at_home, jnp.logical_and(section == p, line == home(p)))
    begin = jnp.where(at_home, skew * (sections - 1 - section), steps)
    on_top = jnp.logical_and(at_home, section >= sections - len(top))
    plan = jnp.stack([begin, section == sections - 1, line, on_top]).astype(jnp.int32)

    (pack,) = call(
        pack_kernel,
        "pack",
        [bf16((2 * rows + up_weights.shape[1] * (wide // width), width))],
        [lengths],
        scratch=[pltpu.VMEM((row_count, width), jnp.bfloat16)] * 2 + [pltpu.SemaphoreType.DMA((2 + wide // width,))],
        loose=[x_saved[0], cotangent, up_weights[0]],
    )
    packs = to_home(pack)

    def placed(parts, turned):
        (turned,) = call(
            functools.partial(place_kernel, parts, [len(down_sources[part]) for part in parts], lines),
            "place",
            [bf16((width, wide))],
            [plan, turned],
            scratch=[pltpu.VMEM((len(parts), block, width), jnp.bfloat16), pltpu.SemaphoreType.DMA((len(parts),))],
            aliases={1: 0},
            loose=[source for part in parts for source in down_sources[part]],
        )
        return turned

    down_sources = [[down_weights[0]]]
    down_turned = placed([0], jnp.zeros((width, wide), jnp.bfloat16))
    down_relay = None
    if relayed:
        out = [(route(p, relayed)[0], route(p, relayed)[0] - detour * lines) for p in top]
        on = [(source, route(p, relayed)[1]) for p, (_, source) in zip(top, out)]
        down_relay = lax.ppermute(down_weights[0], axes, out)
        down_relay = lax.ppermute(down_relay, axes, on)
    down_sources += [[down] for down in to_home(down_weights[0], after=packs)[1:]]
    if relayed:
        down_sources[relayed].append(down_relay)

    act, rise, x_all, store, up_turned = call(
        functools.partial(hidden_kernel, lines, rows),
        "hidden",
        [bf16((total_rows, wide))] * 2 + [bf16((total_rows, width))] * 2 + [bf16((wide, width))],
        [plan, norm_gain],
        scratch=[
            pltpu.VMEM((width, wide), jnp.bfloat16),
            pltpu.VMEM((total_rows, width), jnp.bfloat16),
            pltpu.SemaphoreType.DMA((lines, 2 + wide // width)),
        ],
        loose=packs,
    )
    for index in range(1, lines, 3):
        down_turned = placed(list(range(index, min(index + 3, lines))), down_turned)

    total = jnp.zeros((1, width), jnp.float32)
    arrived = [jnp.zeros((piece_rows, width), jnp.bfloat16)] * skew
    for step in range(steps):
        back, store, total = call(
            functools.partial(chain_kernel, step, piece_rows),
            "chain",
            [bf16((piece_rows, width)), bf16((total_rows, width)), jax.ShapeDtypeStruct((1, width), jnp.float32)],
            [plan, arrived.pop(0), norm_gain, layer_scale, x_all, rise, up_turned, down_turned, store, total],
            scratch=[pltpu.VMEM((piece_rows, wide), jnp.bfloat16), pltpu.VMEM((piece_rows, width), jnp.float32)],
            aliases={8: 1, 9: 2},
        )
        moving = [p for p in range(1, sections) if 0 <= step - skew * (sections - 1 - p) < pieces]
        if moving:
            back = lax.ppermute(back, axes, [(device(p, home(p)), device(p - 1, home(p - 1))) for p in moving])
        arrived.append(back)

    scale_total = jnp.zeros((1, width), jnp.float32)
    weight_total = None
    for part in sorted(range(lines), key=lambda part: -min(part, lines - part)):
        grad, scale_part = call(
            functools.partial(weight_kernel, part, lines),
            "weight",
            [bf16((block, width)), jax.ShapeDtypeStruct((1, width), jnp.float32)],
            [plan, layer_scale, act, store],
            scratch=[pltpu.VMEM((block, width), jnp.bfloat16), pltpu.SemaphoreType.DMA],
            loose=down_sources[part],
        )
        grad = from_home(grad, part) if part else jnp.where(at_home, grad, jnp.zeros_like(grad))
        weight_total = grad if weight_total is None else weight_total + grad
        scale_total = scale_total + scale_part
    sums = jnp.concatenate([total, scale_total], axis=0)
    spread = jnp.where(at_home, sums, jnp.zeros_like(sums))
    for part in range(1, lines):
        spread = spread + from_home(sums, part)
    return (weight_total[None], spread[0:1], spread[1:2])


def solution(mesh):
    return jax.shard_map(
        shards,
        mesh=mesh,
        in_specs=(
            P("pipe", "dp", None),
            P("pipe", "dp", None),
            P("pipe", "dp", None),
            P("pipe", None),
            P("pipe", None),
            P("dp", None),
            P("dp", None),
        ),
        out_specs=(P("pipe", "dp", None), P("pipe", None), P("pipe", None)),
        check_vma=False,
    )
```
